32 devices in a mesh: subj: 8 (over z, y), slab: 4 (over x, core).
Axes of the slice: x: 2, y: 2, z: 4, core: 2. Of those that a mesh axis runs over, the one named last changes fastest.
Arguments:
- image: float32 [8, 192, 8, 192], P('subj', 'slab'), may hold values from -6 to 6
- velocity: float32 [8, 3, 192, 8, 192], P('subj', None, 'slab'), may hold values from -3 to 3
- template: float32 [192, 8, 192], P('slab', 'subj'), may hold values from -6 to 6
- z_kernel: float32 [192, 192], replicated, as said below
- x_kernel: float32 [192, 192], replicated, as said below
Outputs:
- velocity_update: float32 [8, 3, 192, 8, 192], P('subj', None, 'slab')
- new_template: float32 [192, 8, 192], P('slab', 'subj')
The draws below stay inside these ranges and needn't reach their ends.
Inputs may be any that keep to these rules, and one draw needn't show every extreme that they name: `z_kernel`: entries are positive. `x_kernel`: entries are positive.
All inputs are finite; a program needn't handle non-finite values.
Results may differ from the reference program's by a relative error of at most 0.00028.
Values sent between devices are 32-bit elements; how exact they have to be, the bound alone decides.
A program may use at most 64 MiB of HBM per device.

```python
import math
import jax
import jax.numpy as jnp
from jax import lax

NZ = 192
NX = 192
SUBJECTS = 8
YW = 8


def kernel_draw(key, length):
    indices = jnp.arange(length, dtype=jnp.float32)
    distance = jnp.abs(indices[:, None] - indices[None, :])
    factor = jax.random.uniform(key, (length, length), jnp.float32, 0.5, 1.5)
    return jnp.exp(-distance * 4.0 / length) * factor * (2.0 / math.sqrt(length))


def draw_z_kernel(key, part):
    return kernel_draw(jax.random.fold_in(key, 11), NZ)


def draw_x_kernel(key, part):
    return kernel_draw(jax.random.fold_in(key, 23), NX)


def level_of(stream_key, extent, cuts, least, largest):
    loudness, own = 1.0, jax.random.fold_in(stream_key, 6)
    for axis_at, parts in cuts:
        heights = jnp.exp(jax.random.uniform(jax.random.fold_in(own, axis_at), (parts,), jnp.float32, least / len(cuts), largest / len(cuts)))
        loudness = loudness * jnp.repeat(heights, extent[axis_at] // parts).reshape([-1 if axis == axis_at else 1 for axis in range(len(extent))])
    return loudness


def gaussian(stream_key, dims, scale, most, pieces=(), kind=jnp.bfloat16):
    array = scale * jax.random.normal(stream_key, dims, jnp.float32)
    if pieces:
        array = array * level_of(stream_key, dims, pieces, -0.22, 0.18)
    return jnp.clip(array, -most, most).astype(kind)


def setup_inputs(seed: int = 0) -> dict:
    seeds = jax.random.split(jax.random.key(seed), 6)
    image = gaussian(seeds[0], (SUBJECTS, NZ, YW, NX), 1.0, 6.0, ((0, 8), (1, 4)), jnp.float32)
    velocity = gaussian(seeds[1], (SUBJECTS, 3, NZ, YW, NX), 0.5, 3.0, ((0, 8), (2, 4)), jnp.float32)
    template = gaussian(seeds[2], (NZ, YW, NX), 1.0, 6.0, ((0, 4), (1, 8)), jnp.float32)
    z_kernel = draw_z_kernel(jax.random.fold_in(seeds[5], 71), 0)
    x_kernel = draw_x_kernel(jax.random.fold_in(seeds[5], 71), 0)
    return dict(image=image, velocity=velocity, template=template, z_kernel=z_kernel, x_kernel=x_kernel)


def gradients(padded):
    slope_z = (padded[2:, 1:-1, 1:-1] - padded[:-2, 1:-1, 1:-1]) * 0.5
    slope_y = (padded[1:-1, 2:, 1:-1] - padded[1:-1, :-2, 1:-1]) * 0.5
    slope_x = (padded[1:-1, 1:-1, 2:] - padded[1:-1, 1:-1, :-2]) * 0.5
    return jnp.stack([slope_z, slope_y, slope_x])


def reference(image, velocity, template, z_kernel, x_kernel):
    highest = lax.Precision.HIGHEST
    slopes = gradients(jnp.pad(template, 1))

    def per_subject(inputs):
        picture, motion = inputs
        warped = template + jnp.sum(motion * slopes, 0)
        misfit = picture - warped
        forces = misfit[None] * slopes
        along_x = jnp.einsum('czyx,wx->czyw', forces, x_kernel, precision=highest)
        along_z = jnp.einsum('vz,czyw->cvyw', z_kernel, along_x, precision=highest)
        return along_z, misfit

    updates, residuals = lax.map(per_subject, (image, velocity))
    new_template = template + jnp.sum(residuals, 0) / SUBJECTS
    return updates, new_template
```

```python
import functools

import jax
import jax.numpy as jnp
from jax import lax
from jax.experimental import pallas as pl
from jax.experimental.pallas import tpu as pltpu
from jax.sharding import PartitionSpec as P

MESH = pl.DeviceIdType.MESH


def split(x):
    hi = x.astype(jnp.bfloat16)
    return hi, (x - hi.astype(jnp.float32)).astype(jnp.bfloat16)


def dot(a, b):
    return jnp.dot(a, b, preferred_element_type=jnp.float32)


def x_slope(t):
    zero = jnp.zeros((t.shape[0], 1), t.dtype)
    after = jnp.concatenate([t[:, 1:], zero], axis=1)
    before = jnp.concatenate([zero, t[:, :-1]], axis=1)
    return (after - before) * 0.5


def z_slope(t, low, high):
    after = jnp.concatenate([t[1:], high], axis=0)
    before = jnp.concatenate([low, t[:-1]], axis=0)
    return (after - before) * 0.5


def kernel(
    n_subj, n_slab, dz, nx,
    image, velocity, template, zk, xk, out, new_t,
    img_v, vel_v, row_v, zk_v, xk_v, T, R, E, acc, zs, xs, o_v, nt_v,
    loc, t_recv, r_recv, e_recv, a_recv,
    s1, s2, s3, s4, r3, r4, es, as_,
):
    ny = n_subj
    nz = n_slab * dz
    mirrors = n_slab // 2
    outer = n_subj // 2
    s = lax.axis_index("subj")
    k = lax.axis_index("slab")
    par, so = s % 2, s // 2
    core, km = k % 2, k // 2
    partner = so * 2 + 1 - par
    sib = km * 2 + 1 - core

    cps = [
        pltpu.make_async_copy(template, row_v, loc.at[0]),
        pltpu.make_async_copy(image, img_v, loc.at[1]),
        pltpu.make_async_copy(velocity, vel_v, loc.at[2]),
        pltpu.make_async_copy(zk, zk_v, loc.at[3]),
        pltpu.make_async_copy(xk, xk_v, loc.at[4]),
    ]
    for c in cps:
        c.start()

    E[...] = jnp.zeros_like(E)
    T[0] = jnp.zeros_like(T[0])
    T[ny + 1] = jnp.zeros_like(T[ny + 1])

    barrier = pltpu.get_barrier_semaphore()

    def hello(ds, dk):
        pl.semaphore_signal(barrier, inc=1, device_id={"subj": ds, "slab": dk}, device_id_type=MESH)

    for i in range(1, n_subj):
        hello((s + i) % n_subj, k)
    for i in range(n_subj):
        @pl.when(k > 0)
        def _():
            hello((s + i) % n_subj, k - 1)

        @pl.when(k < n_slab - 1)
        def _():
            hello((s + i) % n_subj, k + 1)
    for j in range(n_slab):
        @pl.when((j != k) & (j != k - 1) & (j != k + 1) & ((j % 2 == core) | (j == sib)))
        def _():
            hello(s, j)

    def rdma(src, dst, ss, rs, ds, dk):
        return pltpu.make_async_remote_copy(
            src_ref=src, dst_ref=dst, send_sem=ss, recv_sem=rs,
            device_id={"subj": ds, "slab": dk}, device_id_type=MESH,
        )

    def edge_up(i):
        d = (s + i) % n_subj
        return rdma(row_v.at[dz - 1], E.at[0, s], es.at[0, i], e_recv.at[0, s], d, k + 1)

    def edge_down(i):
        d = (s + i) % n_subj
        return rdma(row_v.at[0], E.at[1, s], es.at[1, i], e_recv.at[1, s], d, k - 1)

    def send1(i):
        d = ((so + i) % outer) * 2 + par
        return rdma(T.at[s + 1, k], T.at[s + 1, k], s1.at[i], t_recv.at[s, k], d, k)

    def send2(y):
        return rdma(T.at[y + 1, k], T.at[y + 1, k], s2.at[y // 2], t_recv.at[y, k], partner, k)

    def send3(y, m):
        dk = ((km + m) % mirrors) * 2 + core
        return rdma(T.at[y + 1, k], T.at[y + 1, k], s3.at[y, m], t_recv.at[y, k], s, dk)

    def send4(y, m):
        kk = ((km + m) % mirrors) * 2 + core
        return rdma(T.at[y + 1, kk], T.at[y + 1, kk], s4.at[y, m], t_recv.at[y, kk], s, sib)

    def got_t(y, kk):
        rdma(T.at[y + 1, kk], T.at[y + 1, kk], s4.at[0, 0], t_recv.at[y, kk], s, sib).wait_recv()

    def rsend3(y, m):
        dk = ((km + m) % mirrors) * 2 + core
        return rdma(R.at[y, k], R.at[y, k], r3.at[y, m], r_recv.at[y, k], s, dk)

    def rsend4(y, m):
        kk = ((km + m) % mirrors) * 2 + core
        return rdma(R.at[y, kk], R.at[y, kk], r4.at[y, m], r_recv.at[y, kk], s, sib)

    def got_r(y, kk):
        rdma(R.at[y, kk], R.at[y, kk], r4.at[0, 0], r_recv.at[y, kk], s, sib).wait_recv()

    def asend(y):
        return rdma(R.at[y, k], acc.at[s], as_.at[y], a_recv.at[s], y, k)

    cps[0].wait()
    T[s + 1, k] = row_v[:, 0, :]

    n_hello = n_subj - 1
    for j in range(n_slab):
        @pl.when(j == k)
        def _():
            near = [i for i in (j - 1, j + 1) if 0 <= i < n_slab]
            far = [i for i in range(n_slab) if i != j and i not in near and (i % 2 == j % 2 or i == (j ^ 1))]
            pl.semaphore_wait(barrier, n_hello + n_subj * len(near) + len(far))

    for i in range(1, outer):
        send1(i).start()
    send2(s).start()
    for i in range(n_subj):
        @pl.when(k < n_slab - 1)
        def _():
            edge_up(i).start()

        @pl.when(k > 0)
        def _():
            edge_down(i).start()

    def spread(y):
        for m in range(1, mirrors):
            send3(y, m).start()
        send4(y, 0).start()

    spread(s)
    for i in range(1, outer):
        y = ((so + i) % outer) * 2 + par
        got_t(y, k)
        send2(y).start()
        spread(y)
    for i in range(outer):
        y = ((so + i) % outer) * 2 + 1 - par
        got_t(y, k)
        spread(y)

    def wait_edge(side):
        def body(y, _):
            rdma(row_v.at[0], E.at[side, y], es.at[0, 0], e_recv.at[side, y], s, k).wait_recv()
            return 0
        lax.fori_loop(0, ny, body, 0)

    @pl.when(k > 0)
    def _():
        wait_edge(0)

    @pl.when(k < n_slab - 1)
    def _():
        wait_edge(1)

    cps[1].wait()
    cps[2].wait()

    def residual(y, _):
        t = T[y + 1, k]
        sz = z_slope(t, E[0, y], E[1, y])
        sy = (T[y + 2, k] - T[y, k]) * 0.5
        sx = x_slope(t)
        rows = pl.ds(y, dz, stride=ny)

        def pick(ref):
            return jnp.concatenate([h[rows, :] for h in ref], axis=1)

        v = [vel_v[c, :, y, :] for c in range(3)]
        r = img_v[:, y, :] - (t + (v[0] * sz + v[1] * sy + v[2] * sx))
        R[y, k] = r
        for m in range(1, mirrors):
            rsend3(y, m).start()
        rsend4(y, 0).start()

        @pl.when(y != s)
        def _():
            asend(y).start()
        return 0

    lax.fori_loop(0, ny, residual, 0)

    cps[3].wait()
    cps[4].wait()
    for j in range(n_slab):
        @pl.when(j == k)
        def _():
            hi, lo = split(zk_v[j * dz:(j + 1) * dz, :])
            zs[0] = hi
            zs[1] = lo
    hi, lo = split(xk_v[...].T)
    xs[0] = hi
    xs[1] = lo

    def mirror_t(y, _):
        for m in range(1, mirrors):
            got_t(y, ((km + m) % mirrors) * 2 + core)
            send4(y, m).start()
        return 0

    lax.fori_loop(0, ny, mirror_t, 0)

    def sibling_t(y, _):
        for m in range(mirrors):
            got_t(y, m * 2 + 1 - core)
        return 0

    lax.fori_loop(0, ny, sibling_t, 0)

    def mirror_r(y):
        for m in range(1, mirrors):
            got_r(y, ((km + m) % mirrors) * 2 + core)
            rsend4(y, m).start()

    def smooth(y):
        for m in range(mirrors):
            got_r(y, m * 2 + 1 - core)
        whole = (nz, nx)
        t = T[y + 1].reshape(whole)
        zero = jnp.zeros((1, nx), jnp.float32)
        r = R[y].reshape(whole)
        slopes = (
            z_slope(t, zero, zero),
            (T[y + 2].reshape(whole) - T[y].reshape(whole)) * 0.5,
            x_slope(t),
        )
        zh, zl = zs[0], zs[1]
        xh, xl = xs[0], xs[1]
        for c in range(3):
            fh, fl = split(r * slopes[c])
            a = dot(zh, fh) + (dot(zh, fl) + dot(zl, fh))
            ah, al = split(a)
            o_v[c, :, y, :] = dot(ah, xh) + (dot(ah, xl) + dot(al, xh))

    mirror_r(0)

    def steps(y, _):
        @pl.when(y + 1 < ny)
        def _():
            mirror_r(y + 1)
        smooth(y)
        return 0

    lax.fori_loop(0, ny, steps, 0)
    o_cp = pltpu.make_async_copy(o_v, out, loc.at[5])
    o_cp.start()

    total = R[s, k]
    for i in range(1, n_subj):
        j = (s + i) % n_subj
        rdma(R.at[0, 0], acc.at[j], as_.at[0], a_recv.at[j], s, k).wait_recv()
        total = total + acc[j]
    nt_v[:, 0, :] = T[s + 1, k] + total / n_subj
    n_cp = pltpu.make_async_copy(nt_v, new_t, loc.at[6])
    n_cp.start()

    for i in range(1, outer):
        send1(i).wait_send()
    for i in range(outer):
        send2(((so + i) % outer) * 2 + par).wait_send()

    def drain(y, _):
        for m in range(1, mirrors):
            send3(y, m).wait_send()
            rsend3(y, m).wait_send()
        for m in range(mirrors):
            send4(y, m).wait_send()
            rsend4(y, m).wait_send()

        @pl.when(y != s)
        def _():
            asend(y).wait_send()

        @pl.when(k < n_slab - 1)
        def _():
            edge_up(y).wait_send()

        @pl.when(k > 0)
        def _():
            edge_down(y).wait_send()
        return 0

    lax.fori_loop(0, ny, drain, 0)
    o_cp.wait()
    n_cp.wait()


def per_device(image, velocity, template, z_kernel, x_kernel):
    n_subj, n_slab = lax.axis_size("subj"), lax.axis_size("slab")
    _, dz, ny, nx = image.shape
    nz = n_slab * dz
    mirrors, outer = n_slab // 2, n_subj // 2
    f32, bf16 = jnp.float32, jnp.bfloat16
    dma = pltpu.SemaphoreType.DMA
    any_ = pl.BlockSpec(memory_space=pl.ANY)
    update, new_template = pl.pallas_call(
        functools.partial(kernel, n_subj, n_slab, dz, nx),
        out_shape=(
            jax.ShapeDtypeStruct((3, dz, ny, nx), f32),
            jax.ShapeDtypeStruct(template.shape, f32),
        ),
        in_specs=[any_] * 5,
        out_specs=(any_, any_),
        scratch_shapes=[
            pltpu.VMEM((dz, ny, nx), f32),
            pltpu.VMEM((3, dz, ny, nx), f32),
            pltpu.VMEM((dz, 1, nx), f32),
            pltpu.VMEM((nz, nz), f32),
            pltpu.VMEM((nx, nx), f32),
            pltpu.VMEM((ny + 2, n_slab, dz, nx), f32),
            pltpu.VMEM((ny, n_slab, dz, nx), f32),
            pltpu.VMEM((2, ny, 1, nx), f32),
            pltpu.VMEM((ny, dz, nx), f32),
            pltpu.VMEM((2, dz, nz), bf16),
            pltpu.VMEM((2, nx, nx), bf16),
            pltpu.VMEM((3, dz, ny, nx), f32),
            pltpu.VMEM((dz, 1, nx), f32),
            dma((7,)),
            dma((ny, n_slab)),
            dma((ny, n_slab)),
            dma((2, ny)),
            dma((ny,)),
            dma((outer,)),
            dma((outer,)),
            dma((ny, mirrors)),
            dma((ny, mirrors)),
            dma((ny, mirrors)),
            dma((ny, mirrors)),
            dma((2, ny)),
            dma((ny,)),
        ],
        compiler_params=pltpu.CompilerParams(
            collective_id=0, has_side_effects=True, vmem_limit_bytes=56 * 1024 * 1024
        ),
    )(image[0], velocity[0], template, z_kernel, x_kernel)
    return update[None], new_template


def solution(mesh):
    in_specs = (
        P("subj", "slab", None, None),
        P("subj", None, "slab", None, None),
        P("slab", "subj", None),
        P(),
        P(),
    )
    out_specs = (P("subj", None, "slab", None, None), P("slab", "subj", None))
    return jax.shard_map(
        per_device, mesh=mesh, in_specs=in_specs, out_specs=out_specs, check_vma=False
    )
```

```python
import functools

import jax
import jax.numpy as jnp
from jax import lax
from jax.experimental import pallas as pl
from jax.experimental.pallas import tpu as pltpu
from jax.sharding import PartitionSpec as P

MESH = pl.DeviceIdType.MESH


def split(x):
    hi = x.astype(jnp.bfloat16)
    return hi, (x - hi.astype(jnp.float32)).astype(jnp.bfloat16)


def dot(a, b):
    return jnp.dot(a, b, preferred_element_type=jnp.float32)


def pack(x):
    dz, nx = x.shape
    rem = nx % 128
    fold = 128 // rem
    step = dz // fold
    tail = x[:, nx - rem:]
    parts = [tail[i * step:(i + 1) * step] for i in range(fold)]
    return jnp.concatenate([x[:, :128], jnp.concatenate(parts, axis=1)], axis=0)


def unpack(x, dz, nx):
    rem = nx % 128
    fold = 128 // rem
    tail = x[..., dz:, :]
    parts = [tail[..., i * rem:(i + 1) * rem] for i in range(fold)]
    tail = jnp.concatenate(parts, axis=-2)
    x = jnp.concatenate([x[..., :dz, :], tail], axis=-1)
    return x.reshape(-1, nx)


def x_slope(t):
    zero = jnp.zeros((t.shape[0], 1), t.dtype)
    after = jnp.concatenate([t[:, 1:], zero], axis=1)
    before = jnp.concatenate([zero, t[:, :-1]], axis=1)
    return (after - before) * 0.5


def z_slope(t, low, high):
    after = jnp.concatenate([t[1:], high], axis=0)
    before = jnp.concatenate([low, t[:-1]], axis=0)
    return (after - before) * 0.5


def kernel(
    n_subj, n_slab, dz, nx,
    image, velocity, template, zk, xk, o_v, nt_v,
    img_v, vel_v, row_v, zk_v, xk_v, T, R, S, E, acc, zs, xs,
    loc, in_sem, t_recv, r_recv, e_recv, a_recv,
    s1, s2, s3, s4, r3, r4, es, as_,
):
    ny = n_subj
    nz = n_slab * dz
    mirrors = n_slab // 2
    outer = n_subj // 2
    s = lax.axis_index("subj")
    k = lax.axis_index("slab")
    par, so = s % 2, s // 2
    core, km = k % 2, k // 2
    partner = so * 2 + 1 - par
    sib = km * 2 + 1 - core

    cps = [
        pltpu.make_async_copy(template, row_v, loc.at[0]),
        pltpu.make_async_copy(zk, zk_v, loc.at[1]),
        pltpu.make_async_copy(xk, xk_v, loc.at[2]),
    ]
    for c in cps:
        c.start()

    def row_in(y):
        return [pltpu.make_async_copy(image.at[:, y, :], img_v.at[y], in_sem.at[3, y])] + [
            pltpu.make_async_copy(velocity.at[c, :, y, :], vel_v.at[c, y], in_sem.at[c, y])
            for c in range(3)
        ]

    def load_rows(y, _):
        for c in row_in(y):
            c.start()
        return 0

    E[...] = jnp.zeros_like(E)
    T[0] = jnp.zeros_like(T[0])
    T[ny + 1] = jnp.zeros_like(T[ny + 1])

    barrier = pltpu.get_barrier_semaphore()

    def hello(ds, dk):
        pl.semaphore_signal(barrier, inc=1, device_id={"subj": ds, "slab": dk}, device_id_type=MESH)

    for i in range(1, n_subj):
        hello((s + i) % n_subj, k)
    for i in range(n_subj):
        @pl.when(k > 0)
        def _():
            hello((s + i) % n_subj, k - 1)

        @pl.when(k < n_slab - 1)
        def _():
            hello((s + i) % n_subj, k + 1)
    for j in range(n_slab):
        @pl.when((j != k) & (j != k - 1) & (j != k + 1) & ((j % 2 == core) | (j == sib)))
        def _():
            hello(s, j)

    def rdma(src, dst, ss, rs, ds, dk):
        return pltpu.make_async_remote_copy(
            src_ref=src, dst_ref=dst, send_sem=ss, recv_sem=rs,
            device_id={"subj": ds, "slab": dk}, device_id_type=MESH,
        )

    def edge_up(i):
        d = (s + i) % n_subj
        return rdma(row_v.at[dz - 1], E.at[0, s], es.at[0, i], e_recv.at[0, s], d, k + 1)

    def edge_down(i):
        d = (s + i) % n_subj
        return rdma(row_v.at[0], E.at[1, s], es.at[1, i], e_recv.at[1, s], d, k - 1)

    def send1(i):
        d = ((so + i) % outer) * 2 + par
        return rdma(T.at[s + 1, k], T.at[s + 1, k], s1.at[i], t_recv.at[s, k], d, k)

    def slab_of(m):
        return ((km + m) % mirrors) * 2 + core

    def send2(y, m):
        kk = slab_of(m)
        return rdma(T.at[y + 1, kk], T.at[y + 1, kk], s2.at[y // 2, m], t_recv.at[y, kk], partner, k)

    def send3(y, m):
        dk = slab_of(m)
        return rdma(T.at[y + 1, k], T.at[y + 1, k], s3.at[y // 2, m], t_recv.at[y, k], s, dk)

    def send4(y, m):
        kk = slab_of(m)
        return rdma(T.at[y + 1, kk], T.at[y + 1, kk], s4.at[y, m], t_recv.at[y, kk], s, sib)

    def got_t(y, kk):
        rdma(T.at[y + 1, kk], T.at[y + 1, kk], s4.at[0, 0], t_recv.at[y, kk], s, sib).wait_recv()

    def rsend3(y, m):
        dk = slab_of(m)
        return rdma(R.at[y, k], R.at[y, k], r3.at[y, m], r_recv.at[y, k], s, dk)

    def rsend4(y, m):
        kk = slab_of(m)
        return rdma(R.at[y, kk], R.at[y, kk], r4.at[y, m], r_recv.at[y, kk], s, sib)

    def got_r(y, kk):
        rdma(R.at[y, kk], R.at[y, kk], r4.at[0, 0], r_recv.at[y, kk], s, sib).wait_recv()

    def asend(y):
        return rdma(R.at[y, k], acc.at[s], as_.at[y], a_recv.at[s], y, k)

    cps[0].wait()
    T[s + 1, k] = pack(row_v[:, 0, :])

    n_hello = n_subj - 1
    for j in range(n_slab):
        @pl.when(j == k)
        def _():
            near = [i for i in (j - 1, j + 1) if 0 <= i < n_slab]
            far = [i for i in range(n_slab) if i != j and i not in near and (i % 2 == j % 2 or i == (j ^ 1))]
            pl.semaphore_wait(barrier, n_hello + n_subj * len(near) + len(far))

    for i in range(1, outer):
        send1(i).start()
    send2(s, 0).start()
    for i in range(n_subj):
        @pl.when(k < n_slab - 1)
        def _():
            edge_up(i).start()

        @pl.when(k > 0)
        def _():
            edge_down(i).start()

    for m in range(1, mirrors):
        send3(s, m).start()
    lax.fori_loop(0, ny, load_rows, 0)
    send4(s, 0).start()
    for i in range(1, outer):
        y = ((so + i) % outer) * 2 + par
        got_t(y, k)
        send2(y, 0).start()
        for m in range(1, mirrors):
            send3(y, m).start()
        send4(y, 0).start()
    for i in range(outer):
        y = ((so + i) % outer) * 2 + 1 - par
        got_t(y, k)
        send4(y, 0).start()

    def wait_edge(side):
        def body(y, _):
            rdma(row_v.at[0], E.at[side, y], es.at[0, 0], e_recv.at[side, y], s, k).wait_recv()
            return 0
        lax.fori_loop(0, ny, body, 0)

    @pl.when(k > 0)
    def _():
        wait_edge(0)

    @pl.when(k < n_slab - 1)
    def _():
        wait_edge(1)

    def residual(y, _):
        t = unpack(T[y + 1, k], dz, nx)
        sz = z_slope(t, E[0, y], E[1, y])
        sy = unpack((T[y + 2, k] - T[y, k]) * 0.5, dz, nx)
        sx = x_slope(t)
        for c in row_in(y):
            c.wait()
        v = [vel_v[c, y] for c in range(3)]
        R[y, k] = pack(img_v[y] - (t + (v[0] * sz + v[1] * sy + v[2] * sx)))
        for m in range(1, mirrors):
            rsend3(y, m).start()
        rsend4(y, 0).start()

        @pl.when(y != s)
        def _():
            asend(y).start()

        @pl.when(y < outer)
        def _():
            yy = ((so + y) % outer) * 2 + par
            for m in range(1, mirrors):
                got_t(yy, slab_of(m))
                send2(yy, m).start()
                send4(yy, m).start()
        return 0

    lax.fori_loop(0, ny, residual, 0)

    cps[1].wait()
    cps[2].wait()
    for j in range(n_slab):
        @pl.when(j == k)
        def _():
            hi, lo = split(zk_v[j * dz:(j + 1) * dz, :])
            zs[0] = hi
            zs[1] = lo
    hi, lo = split(xk_v[...].T)
    xs[0] = hi
    xs[1] = lo

    for i in range(outer):
        y = ((so + i) % outer) * 2 + 1 - par
        for m in range(1, mirrors):
            got_t(y, slab_of(m))
            send4(y, m).start()

    def sibling_t(y, _):
        for m in range(mirrors):
            got_t(y, m * 2 + 1 - core)
        return 0

    lax.fori_loop(0, ny, sibling_t, 0)

    def slopes(y, _):
        zero = jnp.zeros((1, nx), jnp.float32)
        t = unpack(T[y + 1], dz, nx)
        S[y, 0] = z_slope(t, zero, zero)
        S[y, 1] = unpack((T[y + 2] - T[y]) * 0.5, dz, nx)
        S[y, 2] = x_slope(t)
        return 0

    lax.fori_loop(0, ny, slopes, 0)

    def mirror_r(y):
        for m in range(1, mirrors):
            got_r(y, slab_of(m))
            rsend4(y, m).start()

    def smooth(y):
        for m in range(mirrors):
            got_r(y, m * 2 + 1 - core)
        r = unpack(R[y], dz, nx)
        zh, zl = zs[0], zs[1]
        xh, xl = xs[0], xs[1]
        for c in range(3):
            fh, fl = split(r * S[y, c])
            a = dot(zh, fh) + (dot(zh, fl) + dot(zl, fh))
            ah, al = split(a)
            o_v[c, :, y, :] = dot(ah, xh) + (dot(ah, xl) + dot(al, xh))

    mirror_r(0)

    def steps(y, _):
        @pl.when(y + 1 < ny)
        def _():
            mirror_r(y + 1)
        smooth(y)
        return 0

    lax.fori_loop(0, ny, steps, 0)
    total = R[s, k]
    for i in range(1, n_subj):
        j = (s + i) % n_subj
        rdma(R.at[0, 0], acc.at[j], as_.at[0], a_recv.at[j], s, k).wait_recv()
        total = total + acc[j]
    nt_v[:, 0, :] = unpack(T[s + 1, k] + total / n_subj, dz, nx)

    for i in range(1, outer):
        send1(i).wait_send()
    for i in range(outer):
        y = i * 2 + par
        for m in range(mirrors):
            send2(y, m).wait_send()
        for m in range(1, mirrors):
            send3(y, m).wait_send()

    def drain(y, _):
        for m in range(1, mirrors):
            rsend3(y, m).wait_send()
        for m in range(mirrors):
            send4(y, m).wait_send()
            rsend4(y, m).wait_send()

        @pl.when(y != s)
        def _():
            asend(y).wait_send()

        @pl.when(k < n_slab - 1)
        def _():
            edge_up(y).wait_send()

        @pl.when(k > 0)
        def _():
            edge_down(y).wait_send()
        return 0

    lax.fori_loop(0, ny, drain, 0)

def write_out(a, b, out, new_t, sems):
    copies = [pltpu.make_async_copy(a, out, sems.at[0]), pltpu.make_async_copy(b, new_t, sems.at[1])]
    for c in copies:
        c.start()
    for c in copies:
        c.wait()


def per_device(image, velocity, template, z_kernel, x_kernel):
    n_subj, n_slab = lax.axis_size("subj"), lax.axis_size("slab")
    _, dz, ny, nx = image.shape
    nz = n_slab * dz
    mirrors, outer = n_slab // 2, n_subj // 2
    f32, bf16 = jnp.float32, jnp.bfloat16
    dma = pltpu.SemaphoreType.DMA
    any_ = pl.BlockSpec(memory_space=pltpu.HBM)
    vmem = pl.BlockSpec(memory_space=pltpu.VMEM)
    pr = dz + dz * (nx % 128) // 128
    whole = (3, dz, ny, nx)
    a, b = pl.pallas_call(
        functools.partial(kernel, n_subj, n_slab, dz, nx),
        out_shape=(pltpu.VMEM(whole, f32), pltpu.VMEM(template.shape, f32)),
        in_specs=[any_] * 5,
        out_specs=(vmem, vmem),
        scratch_shapes=[
            pltpu.VMEM((ny, dz, nx), f32),
            pltpu.VMEM((3, ny, dz, nx), f32),
            pltpu.VMEM((dz, 1, nx), f32),
            pltpu.VMEM((nz, nz), f32),
            pltpu.VMEM((nx, nx), f32),
            pltpu.VMEM((ny + 2, n_slab, pr, 128), f32),
            pltpu.VMEM((ny, n_slab, pr, 128), f32),
            pltpu.VMEM((ny, 3, nz, nx), f32),
            pltpu.VMEM((2, ny, 1, nx), f32),
            pltpu.VMEM((ny, pr, 128), f32),
            pltpu.VMEM((2, dz, nz), bf16),
            pltpu.VMEM((2, nx, nx), bf16),
            dma((3,)),
            dma((4, ny)),
            dma((ny, n_slab)),
            dma((ny, n_slab)),
            dma((2, ny)),
            dma((ny,)),
            dma((outer,)),
            dma((outer, mirrors)),
            dma((outer, mirrors)),
            dma((ny, mirrors)),
            dma((ny, mirrors)),
            dma((ny, mirrors)),
            dma((2, ny)),
            dma((ny,)),
        ],
        compiler_params=pltpu.CompilerParams(
            collective_id=0, has_side_effects=True, vmem_limit_bytes=56 * 1024 * 1024
        ),
    )(image[0], velocity[0], template, z_kernel, x_kernel)
    update, new_template = pl.pallas_call(
        write_out,
        out_shape=(jax.ShapeDtypeStruct(whole, f32), jax.ShapeDtypeStruct(template.shape, f32)),
        in_specs=[vmem] * 2,
        out_specs=(any_, any_),
        scratch_shapes=[dma((2,))],
    )(a, b)
    return update[None], new_template


def solution(mesh):
    in_specs = (
        P("subj", "slab", None, None),
        P("subj", None, "slab", None, None),
        P("slab", "subj", None),
        P(),
        P(),
    )
    out_specs = (P("subj", None, "slab", None, None), P("slab", "subj", None))
    return jax.shard_map(
        per_device, mesh=mesh, in_specs=in_specs, out_specs=out_specs, check_vma=False
    )
```

```python
import functools

import jax
import jax.numpy as jnp
from jax import lax
from jax.experimental import pallas as pl
from jax.experimental.pallas import tpu as pltpu
from jax.sharding import PartitionSpec as P

MESH = pl.DeviceIdType.MESH


def split(x):
    hi = x.astype(jnp.bfloat16)
    return hi, (x - hi.astype(jnp.float32)).astype(jnp.bfloat16)


def dot(a, b):
    return jnp.dot(a, b, preferred_element_type=jnp.float32)


def pack(x):
    dz, nx = x.shape
    rem = nx % 128
    fold = 128 // rem
    step = dz // fold
    tail = x[:, nx - rem:]
    parts = [tail[i * step:(i + 1) * step] for i in range(fold)]
    return jnp.concatenate([x[:, :128], jnp.concatenate(parts, axis=1)], axis=0)


def unpack(x, dz, nx):
    rem = nx % 128
    fold = 128 // rem
    tail = x[..., dz:, :]
    parts = [tail[..., i * rem:(i + 1) * rem] for i in range(fold)]
    tail = jnp.concatenate(parts, axis=-2)
    x = jnp.concatenate([x[..., :dz, :], tail], axis=-1)
    return x.reshape(-1, nx)


def x_slope(t):
    zero = jnp.zeros((t.shape[0], 1), t.dtype)
    after = jnp.concatenate([t[:, 1:], zero], axis=1)
    before = jnp.concatenate([zero, t[:, :-1]], axis=1)
    return (after - before) * 0.5


def z_slope(t, low, high):
    after = jnp.concatenate([t[1:], high], axis=0)
    before = jnp.concatenate([low, t[:-1]], axis=0)
    return (after - before) * 0.5


def kernel(
    n_subj, n_slab, dz, nx,
    image, velocity, template, zk, z_out, nt_out,
    raw_v, field_v, row_v, zk_v, T, R, S, E, acc, zs, zh, z_v, nt_v,
    loc, in_sem, z_sem, t_recv, r_recv, e_recv, a_recv,
    s1, s2, s3, s4, r3, r4, es, as_,
):
    ny = n_subj
    nz = n_slab * dz
    mirrors = n_slab // 2
    outer = n_subj // 2
    s = lax.axis_index("subj")
    k = lax.axis_index("slab")
    par, so = s % 2, s // 2
    core, km = k % 2, k // 2
    partner = so * 2 + 1 - par
    sib = km * 2 + 1 - core

    cps = [
        pltpu.make_async_copy(template, row_v, loc.at[0]),
        pltpu.make_async_copy(zk, zk_v, loc.at[1]),
    ] + [
        pltpu.make_async_copy(velocity.at[c], raw_v.at[c], in_sem.at[c]) for c in range(3)
    ] + [
        pltpu.make_async_copy(image, raw_v.at[3], in_sem.at[3])
    ]
    for c in cps:
        c.start()

    def transpose(c):
        cps[2 + c].wait()
        field_v[c] = jnp.swapaxes(raw_v[c], 0, 1)

    E[...] = jnp.zeros_like(E)
    T[0] = jnp.zeros_like(T[0])
    T[ny + 1] = jnp.zeros_like(T[ny + 1])

    barrier = pltpu.get_barrier_semaphore()

    def hello(ds, dk):
        pl.semaphore_signal(barrier, inc=1, device_id={"subj": ds, "slab": dk}, device_id_type=MESH)

    for i in range(1, n_subj):
        hello((s + i) % n_subj, k)
    for i in range(n_subj):
        @pl.when(k > 0)
        def _():
            hello((s + i) % n_subj, k - 1)

        @pl.when(k < n_slab - 1)
        def _():
            hello((s + i) % n_subj, k + 1)
    for j in range(n_slab):
        @pl.when((j != k) & (j != k - 1) & (j != k + 1) & ((j % 2 == core) | (j == sib)))
        def _():
            hello(s, j)

    def rdma(src, dst, ss, rs, ds, dk):
        return pltpu.make_async_remote_copy(
            src_ref=src, dst_ref=dst, send_sem=ss, recv_sem=rs,
            device_id={"subj": ds, "slab": dk}, device_id_type=MESH,
        )

    def edge_up(i):
        d = (s + i) % n_subj
        return rdma(row_v.at[dz - 1], E.at[0, s], es.at[0, i], e_recv.at[0, s], d, k + 1)

    def edge_down(i):
        d = (s + i) % n_subj
        return rdma(row_v.at[0], E.at[1, s], es.at[1, i], e_recv.at[1, s], d, k - 1)

    def send1(i):
        d = ((so + i) % outer) * 2 + par
        return rdma(T.at[s + 1, k], T.at[s + 1, k], s1.at[i], t_recv.at[s, k], d, k)

    def slab_of(m):
        return ((km + m) % mirrors) * 2 + core

    def send2(y, m):
        kk = slab_of(m)
        return rdma(T.at[y + 1, kk], T.at[y + 1, kk], s2.at[y // 2, m], t_recv.at[y, kk], partner, k)

    def send3(y, m):
        dk = slab_of(m)
        return rdma(T.at[y + 1, k], T.at[y + 1, k], s3.at[y // 2, m], t_recv.at[y, k], s, dk)

    def send4(y, m):
        kk = slab_of(m)
        return rdma(T.at[y + 1, kk], T.at[y + 1, kk], s4.at[y, m], t_recv.at[y, kk], s, sib)

    def got_t(y, kk):
        rdma(T.at[y + 1, kk], T.at[y + 1, kk], s4.at[0, 0], t_recv.at[y, kk], s, sib).wait_recv()

    def rsend3(y, m):
        dk = slab_of(m)
        return rdma(R.at[y, k], R.at[y, k], r3.at[y, m], r_recv.at[y, k], s, dk)

    def rsend4(y, m):
        kk = slab_of(m)
        return rdma(R.at[y, kk], R.at[y, kk], r4.at[y, m], r_recv.at[y, kk], s, sib)

    def got_r(y, kk):
        rdma(R.at[y, kk], R.at[y, kk], r4.at[0, 0], r_recv.at[y, kk], s, sib).wait_recv()

    def asend(y):
        return rdma(R.at[y, k], acc.at[s], as_.at[y], a_recv.at[s], y, k)

    cps[0].wait()
    T[s + 1, k] = pack(row_v[:, 0, :])

    n_hello = n_subj - 1
    for j in range(n_slab):
        @pl.when(j == k)
        def _():
            near = [i for i in (j - 1, j + 1) if 0 <= i < n_slab]
            far = [i for i in range(n_slab) if i != j and i not in near and (i % 2 == j % 2 or i == (j ^ 1))]
            pl.semaphore_wait(barrier, n_hello + n_subj * len(near) + len(far))

    for i in range(1, outer):
        send1(i).start()
    send2(s, 0).start()
    for i in range(n_subj):
        @pl.when(k < n_slab - 1)
        def _():
            edge_up(i).start()

        @pl.when(k > 0)
        def _():
            edge_down(i).start()

    for m in range(1, mirrors):
        send3(s, m).start()
    send4(s, 0).start()
    transpose(0)
    transpose(1)
    for i in range(1, outer):
        y = ((so + i) % outer) * 2 + par
        got_t(y, k)
        send2(y, 0).start()
        for m in range(1, mirrors):
            send3(y, m).start()
        send4(y, 0).start()
        if i == 1:
            transpose(2)
        if i == 2:
            transpose(3)
    if outer < 3:
        transpose(3)
    for i in range(outer):
        y = ((so + i) % outer) * 2 + 1 - par
        got_t(y, k)
        send4(y, 0).start()

    def wait_edge(side):
        def body(y, _):
            rdma(row_v.at[0], E.at[side, y], es.at[0, 0], e_recv.at[side, y], s, k).wait_recv()
            return 0
        lax.fori_loop(0, ny, body, 0)

    @pl.when(k > 0)
    def _():
        wait_edge(0)

    @pl.when(k < n_slab - 1)
    def _():
        wait_edge(1)

    def residual(y, _):
        t = unpack(T[y + 1, k], dz, nx)
        sz = z_slope(t, E[0, y], E[1, y])
        sy = unpack((T[y + 2, k] - T[y, k]) * 0.5, dz, nx)
        sx = x_slope(t)
        v = [field_v[c, y] for c in range(3)]
        R[y, k] = pack(field_v[3, y] - (t + (v[0] * sz + v[1] * sy + v[2] * sx)))
        for m in range(1, mirrors):
            rsend3(y, m).start()
        rsend4(y, 0).start()

        @pl.when(y != s)
        def _():
            asend(y).start()

        @pl.when(y < outer)
        def _():
            yy = ((so + y) % outer) * 2 + par
            for m in range(1, mirrors):
                got_t(yy, slab_of(m))
                send2(yy, m).start()
                send4(yy, m).start()
        return 0

    lax.fori_loop(0, ny, residual, 0)

    cps[1].wait()
    for j in range(n_slab):
        @pl.when(j == k)
        def _():
            rows = zk_v[j * dz:(j + 1) * dz, :]
            hi = rows.astype(jnp.bfloat16).astype(jnp.float32)
            zs[...] = jnp.concatenate([hi, rows - hi], axis=0).astype(jnp.bfloat16)
            zh[...] = hi.astype(jnp.bfloat16)

    for i in range(outer):
        y = ((so + i) % outer) * 2 + 1 - par
        for m in range(1, mirrors):
            got_t(y, slab_of(m))
            send4(y, m).start()

    def sibling_t(y, _):
        for m in range(mirrors):
            got_t(y, m * 2 + 1 - core)
        return 0

    lax.fori_loop(0, ny, sibling_t, 0)

    def slopes(y, _):
        zero = jnp.zeros((1, nx), jnp.float32)
        t = unpack(T[y + 1], dz, nx)
        S[y, 0] = z_slope(t, zero, zero)
        S[y, 1] = unpack((T[y + 2] - T[y]) * 0.5, dz, nx)
        S[y, 2] = x_slope(t)
        return 0

    lax.fori_loop(0, ny, slopes, 0)

    def mirror_r(y):
        for m in range(1, mirrors):
            got_r(y, slab_of(m))
            rsend4(y, m).start()

    def smooth(y):
        r = unpack(R[y], dz, nx)
        for c in range(3):
            fh, fl = split(r * S[y, c])
            p = dot(zs[...], fh)
            z_v[c, y] = p[:dz] + (p[dz:] + dot(zh[...], fl))

    def z_copy(g):
        part = pl.ds(g * 2, 2)
        return pltpu.make_async_copy(z_v.at[:, part], z_out.at[:, part], z_sem.at[g])

    mirror_r(0)
    mirror_r(1)

    def steps(g, _):
        @pl.when(g + 1 < ny // 2)
        def _():
            mirror_r(2 * g + 2)
            mirror_r(2 * g + 3)
        for i in range(2):
            for m in range(mirrors):
                got_r(2 * g + i, m * 2 + 1 - core)
        for i in range(2):
            smooth(2 * g + i)
        z_copy(g).start()
        return 0

    lax.fori_loop(0, ny // 2, steps, 0)

    total = R[s, k]
    for i in range(1, n_subj):
        j = (s + i) % n_subj
        rdma(R.at[0, 0], acc.at[j], as_.at[0], a_recv.at[j], s, k).wait_recv()
        total = total + acc[j]
    nt_v[:, 0, :] = unpack(T[s + 1, k] + total / n_subj, dz, nx)
    n_cp = pltpu.make_async_copy(nt_v, nt_out, loc.at[2])
    n_cp.start()

    for i in range(1, outer):
        send1(i).wait_send()
    for i in range(outer):
        y = i * 2 + par
        for m in range(mirrors):
            send2(y, m).wait_send()
        for m in range(1, mirrors):
            send3(y, m).wait_send()

    def drain(y, _):
        for m in range(1, mirrors):
            rsend3(y, m).wait_send()
        for m in range(mirrors):
            send4(y, m).wait_send()
            rsend4(y, m).wait_send()

        @pl.when(y != s)
        def _():
            asend(y).wait_send()

        @pl.when(k < n_slab - 1)
        def _():
            edge_up(y).wait_send()

        @pl.when(k > 0)
        def _():
            edge_down(y).wait_send()
        return 0

    lax.fori_loop(0, ny, drain, 0)
    for g in range(ny // 2):
        z_copy(g).wait()
    n_cp.wait()


def smooth_x(z_in, nt_in, xk, out, new_t, z_v, xk_v, o_v, in_sem, out_sem):
    _, ny, dz, nx = z_in.shape
    nt_copy = pltpu.make_async_copy(nt_in, new_t, out_sem.at[3])
    xk_copy = pltpu.make_async_copy(xk, xk_v, in_sem.at[3])
    loads = [pltpu.make_async_copy(z_in.at[c], z_v.at[c], in_sem.at[c]) for c in range(3)]
    stores = [pltpu.make_async_copy(o_v.at[c], out.at[c], out_sem.at[c]) for c in range(3)]
    xk_copy.start()
    for copy in loads:
        copy.start()
    nt_copy.start()
    xk_copy.wait()
    xh, xl = split(xk_v[...].T)
    for c in range(3):
        loads[c].wait()
        ah, al = split(z_v[c].reshape(ny * dz, nx))
        o = dot(ah, xh) + (dot(ah, xl) + dot(al, xh))
        o_v[c] = jnp.swapaxes(o.reshape(ny, dz, nx), 0, 1)
        stores[c].start()
    for copy in stores:
        copy.wait()
    nt_copy.wait()


def per_device(image, velocity, template, z_kernel, x_kernel):
    n_subj, n_slab = lax.axis_size("subj"), lax.axis_size("slab")
    _, dz, ny, nx = image.shape
    nz = n_slab * dz
    mirrors, outer = n_slab // 2, n_subj // 2
    f32, bf16 = jnp.float32, jnp.bfloat16
    dma = pltpu.SemaphoreType.DMA
    any_ = pl.BlockSpec(memory_space=pltpu.HBM)
    pr = dz + dz * (nx % 128) // 128
    by_row = (3, ny, dz, nx)
    whole = (3, dz, ny, nx)
    grant = 56 * 1024 * 1024
    smoothed, updated = pl.pallas_call(
        functools.partial(kernel, n_subj, n_slab, dz, nx),
        out_shape=(
            jax.ShapeDtypeStruct(by_row, f32),
            jax.ShapeDtypeStruct(template.shape, f32),
        ),
        in_specs=[any_] * 4,
        out_specs=(any_, any_),
        scratch_shapes=[
            pltpu.VMEM((4, dz, ny, nx), f32),
            pltpu.VMEM((4, ny, dz, nx), f32),
            pltpu.VMEM((dz, 1, nx), f32),
            pltpu.VMEM((nz, nz), f32),
            pltpu.VMEM((ny + 2, n_slab, pr, 128), f32),
            pltpu.VMEM((ny, n_slab, pr, 128), f32),
            pltpu.VMEM((ny, 3, nz, nx), f32),
            pltpu.VMEM((2, ny, 1, nx), f32),
            pltpu.VMEM((ny, pr, 128), f32),
            pltpu.VMEM((2 * dz, nz), bf16),
            pltpu.VMEM((dz, nz), bf16),
            pltpu.VMEM(by_row, f32),
            pltpu.VMEM((dz, 1, nx), f32),
            dma((3,)),
            dma((4,)),
            dma((ny // 2,)),
            dma((ny, n_slab)),
            dma((ny, n_slab)),
            dma((2, ny)),
            dma((ny,)),
            dma((outer,)),
            dma((outer, mirrors)),
            dma((outer, mirrors)),
            dma((ny, mirrors)),
            dma((ny, mirrors)),
            dma((ny, mirrors)),
            dma((2, ny)),
            dma((ny,)),
        ],
        compiler_params=pltpu.CompilerParams(
            collective_id=0, has_side_effects=True, vmem_limit_bytes=grant
        ),
    )(image[0], velocity[0], template, z_kernel)
    update, new_template = pl.pallas_call(
        smooth_x,
        out_shape=(jax.ShapeDtypeStruct(whole, f32), jax.ShapeDtypeStruct(template.shape, f32)),
        in_specs=[any_] * 3,
        out_specs=(any_, any_),
        scratch_shapes=[
            pltpu.VMEM(by_row, f32),
            pltpu.VMEM((nx, nx), f32),
            pltpu.VMEM(whole, f32),
            dma((4,)),
            dma((4,)),
        ],
        compiler_params=pltpu.CompilerParams(vmem_limit_bytes=grant),
    )(smoothed, updated, x_kernel)
    return update[None], new_template


def solution(mesh):
    in_specs = (
        P("subj", "slab", None, None),
        P("subj", None, "slab", None, None),
        P("slab", "subj", None),
        P(),
        P(),
    )
    out_specs = (P("subj", None, "slab", None, None), P("slab", "subj", None))
    return jax.shard_map(
        per_device, mesh=mesh, in_specs=in_specs, out_specs=out_specs, check_vma=False
    )
```

```python
import functools

import jax
import jax.numpy as jnp
from jax import lax
from jax.experimental import pallas as pl
from jax.experimental.pallas import tpu as pltpu
from jax.sharding import PartitionSpec as P

MESH = pl.DeviceIdType.MESH


def split(x):
    hi = x.astype(jnp.bfloat16)
    return hi, (x - hi.astype(jnp.float32)).astype(jnp.bfloat16)


def dot(a, b):
    return jnp.dot(a, b, preferred_element_type=jnp.float32)


def pack(x):
    dz, nx = x.shape
    rem = nx % 128
    fold = 128 // rem
    step = dz // fold
    tail = x[:, nx - rem:]
    parts = [tail[i * step:(i + 1) * step] for i in range(fold)]
    return jnp.concatenate([x[:, :128], jnp.concatenate(parts, axis=1)], axis=0)


def unpack(x, dz, nx):
    rem = nx % 128
    fold = 128 // rem
    tail = x[..., dz:, :]
    parts = [tail[..., i * rem:(i + 1) * rem] for i in range(fold)]
    tail = jnp.concatenate(parts, axis=-2)
    x = jnp.concatenate([x[..., :dz, :], tail], axis=-1)
    return x.reshape(-1, nx)


def x_slope(t):
    zero = jnp.zeros((t.shape[0], 1), t.dtype)
    after = jnp.concatenate([t[:, 1:], zero], axis=1)
    before = jnp.concatenate([zero, t[:, :-1]], axis=1)
    return (after - before) * 0.5


def z_slope(t, low, high):
    after = jnp.concatenate([t[1:], high], axis=0)
    before = jnp.concatenate([low, t[:-1]], axis=0)
    return (after - before) * 0.5


def kernel(
    n_subj, n_slab, dz, nx,
    image, velocity, template, zk, z_out, nt_out,
    raw_v, field_v, row_v, zk_v, T, R, S, E, acc, zs, zh, z_v, nt_v,
    loc, in_sem, z_sem, t_recv, r_recv, e_recv, a_recv,
    s1, s2, s3, s4, r3, r4, es, as_,
):
    ny = n_subj
    nz = n_slab * dz
    mirrors = n_slab // 2
    outer = n_subj // 2
    s = lax.axis_index("subj")
    k = lax.axis_index("slab")
    par, so = s % 2, s // 2
    core, km = k % 2, k // 2
    partner = so * 2 + 1 - par
    sib = km * 2 + 1 - core

    cps = [
        pltpu.make_async_copy(template, row_v, loc.at[0]),
        pltpu.make_async_copy(zk, zk_v, loc.at[1]),
    ] + [
        pltpu.make_async_copy(velocity.at[c], raw_v.at[c], in_sem.at[c]) for c in range(3)
    ] + [
        pltpu.make_async_copy(image, raw_v.at[3], in_sem.at[3])
    ]
    for c in cps:
        c.start()

    def transpose(c):
        cps[2 + c].wait()
        field_v[c] = jnp.swapaxes(raw_v[c], 0, 1)

    E[...] = jnp.zeros_like(E)
    T[0] = jnp.zeros_like(T[0])
    T[ny + 1] = jnp.zeros_like(T[ny + 1])

    barrier = pltpu.get_barrier_semaphore()

    def hello(ds, dk):
        pl.semaphore_signal(barrier, inc=1, device_id={"subj": ds, "slab": dk}, device_id_type=MESH)

    for i in range(1, n_subj):
        hello((s + i) % n_subj, k)
    for i in range(n_subj):
        @pl.when(k > 0)
        def _():
            hello((s + i) % n_subj, k - 1)

        @pl.when(k < n_slab - 1)
        def _():
            hello((s + i) % n_subj, k + 1)
    for j in range(n_slab):
        @pl.when((j != k) & (j != k - 1) & (j != k + 1) & ((j % 2 == core) | (j == sib)))
        def _():
            hello(s, j)

    def rdma(src, dst, ss, rs, ds, dk):
        return pltpu.make_async_remote_copy(
            src_ref=src, dst_ref=dst, send_sem=ss, recv_sem=rs,
            device_id={"subj": ds, "slab": dk}, device_id_type=MESH,
        )

    def edge_up(i):
        d = (s + i) % n_subj
        return rdma(row_v.at[dz - 1], E.at[0, s], es.at[0, i], e_recv.at[0, s], d, k + 1)

    def edge_down(i):
        d = (s + i) % n_subj
        return rdma(row_v.at[0], E.at[1, s], es.at[1, i], e_recv.at[1, s], d, k - 1)

    def send1(i):
        d = ((so + i) % outer) * 2 + par
        return rdma(T.at[s + 1, k], T.at[s + 1, k], s1.at[i], t_recv.at[s, k], d, k)

    def slab_of(m):
        return ((km + m) % mirrors) * 2 + core

    def send2(y, m):
        kk = slab_of(m)
        return rdma(T.at[y + 1, kk], T.at[y + 1, kk], s2.at[y // 2, m], t_recv.at[y, kk], partner, k)

    def send3(y, m):
        dk = slab_of(m)
        return rdma(T.at[y + 1, k], T.at[y + 1, k], s3.at[y // 2, m], t_recv.at[y, k], s, dk)

    def send4(y, m):
        kk = slab_of(m)
        return rdma(T.at[y + 1, kk], T.at[y + 1, kk], s4.at[y, m], t_recv.at[y, kk], s, sib)

    def got_t(y, kk):
        rdma(T.at[y + 1, kk], T.at[y + 1, kk], s4.at[0, 0], t_recv.at[y, kk], s, sib).wait_recv()

    def rsend3(y, m):
        dk = slab_of(m)
        return rdma(R.at[y, k], R.at[y, k], r3.at[y, m], r_recv.at[y, k], s, dk)

    def rsend4(y, m):
        kk = slab_of(m)
        return rdma(R.at[y, kk], R.at[y, kk], r4.at[y, m], r_recv.at[y, kk], s, sib)

    def got_r(y, kk):
        rdma(R.at[y, kk], R.at[y, kk], r4.at[0, 0], r_recv.at[y, kk], s, sib).wait_recv()

    def asend(y):
        return rdma(R.at[y, k], acc.at[s], as_.at[y], a_recv.at[s], y, k)

    cps[0].wait()
    T[s + 1, k] = pack(row_v[:, 0, :])

    n_hello = n_subj - 1
    for j in range(n_slab):
        @pl.when(j == k)
        def _():
            near = [i for i in (j - 1, j + 1) if 0 <= i < n_slab]
            far = [i for i in range(n_slab) if i != j and i not in near and (i % 2 == j % 2 or i == (j ^ 1))]
            pl.semaphore_wait(barrier, n_hello + n_subj * len(near) + len(far))

    for i in range(1, outer):
        send1(i).start()
    send2(s, 0).start()
    for i in range(n_subj):
        @pl.when(k < n_slab - 1)
        def _():
            edge_up(i).start()

        @pl.when(k > 0)
        def _():
            edge_down(i).start()

    for m in range(1, mirrors):
        send3(s, m).start()
    send4(s, 0).start()
    transpose(0)
    transpose(1)
    for i in range(1, outer):
        y = ((so + i) % outer) * 2 + par
        got_t(y, k)
        send2(y, 0).start()
        for m in range(1, mirrors):
            send3(y, m).start()
        send4(y, 0).start()
        if i == 1:
            transpose(2)
        if i == 2:
            transpose(3)
    if outer < 3:
        transpose(3)
    for i in range(outer):
        y = ((so + i) % outer) * 2 + 1 - par
        got_t(y, k)
        send4(y, 0).start()

    def wait_edge(side):
        def body(y, _):
            rdma(row_v.at[0], E.at[side, y], es.at[0, 0], e_recv.at[side, y], s, k).wait_recv()
            return 0
        lax.fori_loop(0, ny, body, 0)

    @pl.when(k > 0)
    def _():
        wait_edge(0)

    @pl.when(k < n_slab - 1)
    def _():
        wait_edge(1)

    def residual(y, _):
        t = unpack(T[y + 1, k], dz, nx)
        sz = z_slope(t, E[0, y], E[1, y])
        sy = unpack((T[y + 2, k] - T[y, k]) * 0.5, dz, nx)
        sx = x_slope(t)
        v = [field_v[c, y] for c in range(3)]
        R[y, k] = pack(field_v[3, y] - (t + (v[0] * sz + v[1] * sy + v[2] * sx)))
        for m in range(1, mirrors):
            rsend3(y, m).start()
        rsend4(y, 0).start()

        @pl.when(y != s)
        def _():
            asend(y).start()

        @pl.when(y < outer)
        def _():
            yy = ((so + y) % outer) * 2 + par
            for m in range(1, mirrors):
                got_t(yy, slab_of(m))
                send2(yy, m).start()
                send4(yy, m).start()
        return 0

    lax.fori_loop(0, ny, residual, 0)

    cps[1].wait()
    for j in range(n_slab):
        @pl.when(j == k)
        def _():
            rows = zk_v[j * dz:(j + 1) * dz, :]
            hi = rows.astype(jnp.bfloat16).astype(jnp.float32)
            zs[...] = jnp.concatenate([hi, rows - hi], axis=0).astype(jnp.bfloat16)
            zh[...] = hi.astype(jnp.bfloat16)

    for i in range(outer):
        y = ((so + i) % outer) * 2 + 1 - par
        for m in range(1, mirrors):
            got_t(y, slab_of(m))
            send4(y, m).start()

    def sibling_t(y, _):
        for m in range(mirrors):
            got_t(y, m * 2 + 1 - core)
        return 0

    sibling_t(0, 0)

    def mirror_r(y):
        for m in range(1, mirrors):
            got_r(y, slab_of(m))
            rsend4(y, m).start()

    def slopes(y, _):
        @pl.when(y + 1 < ny)
        def _():
            sibling_t(y + 1, 0)
        zero = jnp.zeros((1, nx), jnp.float32)
        t = unpack(T[y + 1], dz, nx)
        S[y, 0] = z_slope(t, zero, zero)
        S[y, 1] = unpack((T[y + 2] - T[y]) * 0.5, dz, nx)
        S[y, 2] = x_slope(t)
        mirror_r(y)
        return 0

    lax.fori_loop(0, ny, slopes, 0)

    def smooth(y):
        r = unpack(R[y], dz, nx)
        for c in range(3):
            fh, fl = split(r * S[y, c])
            p = dot(zs[...], fh)
            z_v[c, y] = p[:dz] + (p[dz:] + dot(zh[...], fl))

    def z_copy(g):
        part = pl.ds(g * 2, 2)
        return pltpu.make_async_copy(z_v.at[:, part], z_out.at[:, part], z_sem.at[g])

    def steps(g, _):
        for i in range(2):
            for m in range(mirrors):
                got_r(2 * g + i, m * 2 + 1 - core)
        for i in range(2):
            smooth(2 * g + i)
        z_copy(g).start()
        return 0

    lax.fori_loop(0, ny // 2, steps, 0)

    total = R[s, k]
    for i in range(1, n_subj):
        j = (s + i) % n_subj
        rdma(R.at[0, 0], acc.at[j], as_.at[0], a_recv.at[j], s, k).wait_recv()
        total = total + acc[j]
    nt_v[:, 0, :] = unpack(T[s + 1, k] + total / n_subj, dz, nx)
    n_cp = pltpu.make_async_copy(nt_v, nt_out, loc.at[2])
    n_cp.start()

    for i in range(1, outer):
        send1(i).wait_send()
    for i in range(outer):
        y = i * 2 + par
        for m in range(mirrors):
            send2(y, m).wait_send()
        for m in range(1, mirrors):
            send3(y, m).wait_send()

    def drain(y, _):
        for m in range(1, mirrors):
            rsend3(y, m).wait_send()
        for m in range(mirrors):
            send4(y, m).wait_send()
            rsend4(y, m).wait_send()

        @pl.when(y != s)
        def _():
            asend(y).wait_send()

        @pl.when(k < n_slab - 1)
        def _():
            edge_up(y).wait_send()

        @pl.when(k > 0)
        def _():
            edge_down(y).wait_send()
        return 0

    lax.fori_loop(0, ny, drain, 0)
    for g in range(ny // 2):
        z_copy(g).wait()
    n_cp.wait()


def smooth_x(z_in, nt_in, xk, out, new_t, z_v, xk_v, o_v, in_sem, out_sem):
    _, ny, dz, nx = z_in.shape
    nt_copy = pltpu.make_async_copy(nt_in, new_t, out_sem.at[3])
    xk_copy = pltpu.make_async_copy(xk, xk_v, in_sem.at[3])
    loads = [pltpu.make_async_copy(z_in.at[c], z_v.at[c], in_sem.at[c]) for c in range(3)]
    stores = [pltpu.make_async_copy(o_v.at[c], out.at[c], out_sem.at[c]) for c in range(3)]
    xk_copy.start()
    for copy in loads:
        copy.start()
    nt_copy.start()
    xk_copy.wait()
    xh, xl = split(xk_v[...].T)
    for c in range(3):
        loads[c].wait()
        ah, al = split(z_v[c].reshape(ny * dz, nx))
        o = dot(ah, xh) + (dot(ah, xl) + dot(al, xh))
        o_v[c] = jnp.swapaxes(o.reshape(ny, dz, nx), 0, 1)
        stores[c].start()
    for copy in stores:
        copy.wait()
    nt_copy.wait()


def per_device(image, velocity, template, z_kernel, x_kernel):
    n_subj, n_slab = lax.axis_size("subj"), lax.axis_size("slab")
    _, dz, ny, nx = image.shape
    nz = n_slab * dz
    mirrors, outer = n_slab // 2, n_subj // 2
    f32, bf16 = jnp.float32, jnp.bfloat16
    dma = pltpu.SemaphoreType.DMA
    any_ = pl.BlockSpec(memory_space=pltpu.HBM)
    pr = dz + dz * (nx % 128) // 128
    by_row = (3, ny, dz, nx)
    whole = (3, dz, ny, nx)
    grant = 56 * 1024 * 1024
    smoothed, updated = pl.pallas_call(
        functools.partial(kernel, n_subj, n_slab, dz, nx),
        out_shape=(
            jax.ShapeDtypeStruct(by_row, f32),
            jax.ShapeDtypeStruct(template.shape, f32),
        ),
        in_specs=[any_] * 4,
        out_specs=(any_, any_),
        scratch_shapes=[
            pltpu.VMEM((4, dz, ny, nx), f32),
            pltpu.VMEM((4, ny, dz, nx), f32),
            pltpu.VMEM((dz, 1, nx), f32),
            pltpu.VMEM((nz, nz), f32),
            pltpu.VMEM((ny + 2, n_slab, pr, 128), f32),
            pltpu.VMEM((ny, n_slab, pr, 128), f32),
            pltpu.VMEM((ny, 3, nz, nx), f32),
            pltpu.VMEM((2, ny, 1, nx), f32),
            pltpu.VMEM((ny, pr, 128), f32),
            pltpu.VMEM((2 * dz, nz), bf16),
            pltpu.VMEM((dz, nz), bf16),
            pltpu.VMEM(by_row, f32),
            pltpu.VMEM((dz, 1, nx), f32),
            dma((3,)),
            dma((4,)),
            dma((ny // 2,)),
            dma((ny, n_slab)),
            dma((ny, n_slab)),
            dma((2, ny)),
            dma((ny,)),
            dma((outer,)),
            dma((outer, mirrors)),
            dma((outer, mirrors)),
            dma((ny, mirrors)),
            dma((ny, mirrors)),
            dma((ny, mirrors)),
            dma((2, ny)),
            dma((ny,)),
        ],
        compiler_params=pltpu.CompilerParams(
            collective_id=0, has_side_effects=True, vmem_limit_bytes=grant
        ),
    )(image[0], velocity[0], template, z_kernel)
    update, new_template = pl.pallas_call(
        smooth_x,
        out_shape=(jax.ShapeDtypeStruct(whole, f32), jax.ShapeDtypeStruct(template.shape, f32)),
        in_specs=[any_] * 3,
        out_specs=(any_, any_),
        scratch_shapes=[
            pltpu.VMEM(by_row, f32),
            pltpu.VMEM((nx, nx), f32),
            pltpu.VMEM(whole, f32),
            dma((4,)),
            dma((4,)),
        ],
        compiler_params=pltpu.CompilerParams(vmem_limit_bytes=grant),
    )(smoothed, updated, x_kernel)
    return update[None], new_template


def solution(mesh):
    in_specs = (
        P("subj", "slab", None, None),
        P("subj", None, "slab", None, None),
        P("slab", "subj", None),
        P(),
        P(),
    )
    out_specs = (P("subj", None, "slab", None, None), P("slab", "subj", None))
    return jax.shard_map(
        per_device, mesh=mesh, in_specs=in_specs, out_specs=out_specs, check_vma=False
    )
```
